128 devices in a mesh: gx: 8 (over z_lo, y), gy: 16 (over x, z_hi, core).
Axes of the slice: x: 4, y: 4, z: 4 (z_hi: 2, z_lo: 2; z = z_hi * 2 + z_lo), core: 2. Of those that a mesh axis runs over, the one named last changes fastest.
Arguments:
- volume: float32 [4, 64, 128, 128], P(None, 'gx', 'gy'), may hold values from -6 to 6
- kernel_one: float32 [16, 4, 3, 3, 3], replicated, may hold values from -0.625 to 0.625
- bias_one: float32 [16], replicated, may hold values from -3 to 3
- kernel_two: float32 [32, 16, 3, 3, 3], replicated, may hold values from -0.3125 to 0.3125
- bias_two: float32 [32], replicated, may hold values from -3 to 3
- cotangent: float32 [32, 16, 1024], P('gy', 'gx'), may hold values from -6 to 6
Outputs:
- pooled: float32 [32, 16, 1024], P('gy', 'gx')
- grad_kernel_one: float32 [16, 4, 3, 3, 3], replicated
- grad_bias_one: float32 [16], replicated
- grad_kernel_two: float32 [32, 16, 3, 3, 3], replicated
- grad_bias_two: float32 [32], replicated
The draws below stay inside these ranges and needn't reach their ends.
All inputs are finite; a program needn't handle non-finite values.
Results may differ from the reference program's by a relative error of at most 0.0003.
Values sent between devices are 32-bit elements; how exact they have to be, the bound alone decides.
No kernel may reach another device: no remote copies, remote signals or barrier semaphores. Data moves between devices by JAX's collectives and lax.ppermute only.
A program may use at most 128 MiB of HBM per device.

```python
import math
import jax
import jax.numpy as jnp
from jax import lax

CIN = 4
C1 = 16
C2 = 32
CX = 8
NX = 64
NY = 128
NZ = 128


def shard_levels(stream_key, dims, shards, low, high):
    level = 1.0
    for dim, parts in shards:
        steps = jax.random.uniform(jax.random.fold_in(jax.random.fold_in(stream_key, 6), dim), (parts,), jnp.float32, low / len(shards), high / len(shards))
        level = level * jnp.repeat(jnp.exp(steps), dims[dim] // parts).reshape((-1,) + (1,) * (len(dims) - 1 - dim))
    return level


def bell_draw(own_key, dims, spread, most, split=(), kind=jnp.bfloat16):
    gain = shard_levels(own_key, dims, split, -0.22, 0.18) if split else 1.0
    values = jax.random.normal(own_key, dims, jnp.float32) * spread * gain
    return jnp.minimum(jnp.maximum(values, -most), most).astype(kind)


def setup_inputs(seed: int = 0) -> dict:
    key_list = jax.random.split(jax.random.key(seed), 7)
    return {
        "volume": bell_draw(key_list[0], (CIN, NX, NY, NZ), 1.0, 6.0, ((1, 8), (2, 16)), jnp.float32),
        "kernel_one": bell_draw(key_list[1], (C1, CIN, 3, 3, 3), (CIN * 27) ** -0.5, 0.625, (), jnp.float32),
        "bias_one": bell_draw(key_list[2], (C1,), 1.0, 3.0, (), jnp.float32),
        "kernel_two": bell_draw(key_list[3], (C2, C1, 3, 3, 3), (C1 * 27) ** -0.5, 0.3125, (), jnp.float32),
        "bias_two": bell_draw(key_list[4], (C2,), 1.0, 3.0, (), jnp.float32),
        "cotangent": bell_draw(key_list[5], (C2, NX // 4, (NY // 4) * (NZ // 4)), 1.0, 6.0, ((0, 16), (1, 8)), jnp.float32),
    }


def convolve(field, kernel, padding):
    result = lax.conv_general_dilated(field[None], kernel, (1, 1, 1), padding, dimension_numbers=('NCDHW', 'OIDHW', 'NCDHW'), precision=lax.Precision.HIGHEST)
    return result[0]

def average_cells(field):
    chans, ext_a, ext_b, ext_c = field.shape
    return field.reshape(chans, ext_a // 2, 2, ext_b // 2, 2, ext_c // 2, 2).mean(axis=(2, 4, 6))

def block_forward(weights, volume_slab, first_row, block_rows):
    kernel_one, bias_one, kernel_two, bias_two = weights
    act_one = convolve(volume_slab, kernel_one, ((0, 0), (1, 1), (1, 1))) + bias_one[:, None, None, None]
    pooled_one = average_cells(jax.nn.silu(act_one))
    row_index = jnp.arange(2 * block_rows + 2, dtype=jnp.int32) + 2 * first_row - 1
    inside = ((row_index >= 0) & (row_index < NX // 2)).astype(pooled_one.dtype)
    pooled_one = pooled_one * inside[None, :, None, None]
    act_two = convolve(pooled_one, kernel_two, ((0, 0), (1, 1), (1, 1))) + bias_two[:, None, None, None]
    return average_cells(jax.nn.silu(act_two))

def reference(volume, kernel_one, bias_one, kernel_two, bias_two, cotangent):
    block_rows = math.gcd(CX // 4, 8)
    block_count = NX // 4 // block_rows
    padded_volume = jnp.pad(volume, ((0, 0), (3, 3), (0, 0), (0, 0)))
    upstream = cotangent.reshape(C2, NX // 4, NY // 4, NZ // 4) * (8.0 / NX)
    weights = (kernel_one, bias_one, kernel_two, bias_two)

    def advance(totals, position):
        first_row = (position * block_rows).astype(jnp.int32)
        volume_slab = lax.dynamic_slice_in_dim(padded_volume, 4 * first_row, 4 * block_rows + 6, 1)

        def forward(values):
            return block_forward(values, volume_slab, first_row, block_rows)
        result, pullback = jax.vjp(forward, weights)
        gradients = pullback(lax.dynamic_slice_in_dim(upstream, first_row, block_rows, 1))[0]
        totals = jax.tree.map(jnp.add, totals, gradients)
        return (totals, result)
    initial = jax.tree.map(jnp.zeros_like, weights)
    gradients, blocks = lax.scan(advance, initial, jnp.arange(block_count, dtype=jnp.int32))
    pooled = jnp.transpose(blocks, (1, 0, 2, 3, 4)).reshape(C2, NX // 4, NY // 4 * (NZ // 4))
    return (pooled, gradients[0], gradients[1], gradients[2], gradients[3])
```

```python
import functools

import jax
import jax.numpy as jnp
from jax import lax
from jax.experimental import pallas as pl
from jax.experimental.pallas import tpu as pltpu
from jax.sharding import PartitionSpec as P

F32, BF16 = jnp.float32, jnp.bfloat16
HALO = 3
TAPS = [(a, b) for a in range(3) for b in range(3)]
NT = (((1,), (1,)), ((), ()))
VMEM = pltpu.CompilerParams(vmem_limit_bytes=56 * 2**20)


def mm(left, right):
    return jnp.dot(left, right, preferred_element_type=F32)


def mm_nt(left, right):
    return lax.dot_general(left, right, NT, preferred_element_type=F32)


def split2(value):
    high = value.astype(BF16)
    return high, (value - high.astype(F32)).astype(BF16)


def split3(value):
    high, rest = split2(value)
    low = value - high.astype(F32) - rest.astype(F32)
    return high, rest, low.astype(BF16)


def iota(shape, dim):
    return lax.broadcasted_iota(jnp.int32, shape, dim)


def lane_shift(value, by):
    axis = value.ndim - 1
    lane = iota(value.shape, axis)
    moved = pltpu.roll(value, by % 128, axis)
    keep = lane >= by if by > 0 else lane < 128 + by
    return jnp.where(keep, moved, 0.0)


def sigmoid(value):
    return 1.0 / (1.0 + jnp.exp(-value))


def eye(size):
    return (iota((size, size), 0) == iota((size, size), 1)).astype(BF16)


def xor_rows(value, bits, rows_per):
    rows = value.shape[0]
    group = iota(value.shape, 0) // rows_per
    for bit in range(4):
        span = rows_per << bit
        upper = (group >> bit) & 1
        swapped = jnp.where(
            upper == 1,
            pltpu.roll(value, span, 0),
            pltpu.roll(value, rows - span, 0),
        )
        value = jnp.where(((bits >> bit) & 1) == 1, swapped, value)
    return value


def prepare(k1, b1, k2, b2, left_one, left_two, left_back):
    def ones_first(bias, rows):
        row = iota((rows, bias.shape[1]), 0)
        return jnp.where(row == 0, jnp.broadcast_to(bias, (rows, bias.shape[1])), 0.0)

    taps = [jnp.concatenate([k1[t], k1[t]], axis=0) for t in range(27)]
    whole = jnp.concatenate(taps + [ones_first(b1[...], 8)], axis=0)
    high, low = split2(whole)
    left_one[0:16, :] = mm_nt(eye(16), high).astype(BF16)
    left_one[16:32, :] = mm_nt(eye(16), low).astype(BF16)
    taps = [jnp.concatenate([k2[t], k2[t]], axis=0) for t in range(27)]
    whole = jnp.concatenate(taps + [ones_first(b2[...], 16)], axis=0)
    high, low = split2(whole)
    left_two[0:32, :] = mm_nt(eye(32), high).astype(BF16)
    left_two[32:64, :] = mm_nt(eye(32), low).astype(BF16)
    for t in range(27):
        high, low = split2(k2[t])
        left_back[16 * t : 16 * t + 16, :] = jnp.concatenate([high, high, low, low], axis=1)


def work(
    place, edge, xlo, own, xhi, ylo, yhi, left_one, left_two, left_back, up,
    map_out, sums,
    s_one, p_one, d_one, s_two, p_two, d_two, y_back, g_one,
):
    scale_up = edge[12]

    def columns(block, x, y):
        high = block.astype(BF16).astype(F32)
        both = jnp.concatenate([high, block - high], axis=1)
        count = block.shape[0]
        s_one[x, y : y + count, 0:8, :] = lane_shift(both, 1)
        s_one[x, y : y + count, 8:16, :] = both
        s_one[x, y : y + count, 16:24, :] = lane_shift(both, -1)

    for ref, start in ((xlo, 0), (own, HALO), (xhi, HALO + own.shape[0])):
        for x in range(ref.shape[0]):
            columns(ref[x], start + x, HALO)
    for x in range(14):
        columns(ylo[x], x, 0)
        columns(yhi[x], x, 11)

    one_row = (iota((8, 128), 0) == 0).astype(F32)
    even = (iota((16, 128), 1) & 1) == 0

    def first(px, carry):
        total = None
        for dx in range(2):
            x = 2 * px + dx
            for y in range(12):
                patch = jnp.concatenate([s_one[x + a, y + b] for a, b in TAPS] + [one_row], axis=0)
                at = pl.multiple_of((x * 12 + y) * 128, 128)
                p_one[:, pl.ds(at, 128)] = patch.astype(BF16)
            at = pl.multiple_of(x * 1536, 1536)
            act = mm(left_one[...], p_one[:, pl.ds(at, 1536)])
            act = act[0:16] + act[16:32]
            gate = sigmoid(act)
            d_one[x] = gate * (1.0 + act * (1.0 - gate))
            total = act * gate if total is None else total + act * gate
        for py in range(6):
            at = 256 * py
            cell = total[:, at : at + 128] + total[:, at + 128 : at + 256]
            cell = cell + pltpu.roll(cell, 127, 1)
            cell = jnp.where(even, cell, 0.0) * (0.125 * edge[px] * edge[6 + py])
            for c, by in enumerate((2, 0, -2)):
                moved = lane_shift(cell, by) if by else cell
                high, low = split2(moved)
                s_two[px, py, 32 * c : 32 * c + 32, :] = jnp.concatenate([high, low], axis=0)
        return carry

    lax.fori_loop(0, 6, first, 0)

    ones_rows = (iota((16, 128), 0) == 0).astype(F32).astype(BF16)
    cells = []
    for x in range(4):
        for y in range(4):
            at = (x * 4 + y) * 128
            for t, (a, b) in enumerate(TAPS):
                p_two[96 * t : 96 * t + 96, at : at + 128] = s_two[x + a, y + b]
            p_two[864:880, at : at + 128] = ones_rows
        act = mm(left_two[...], p_two[:, 512 * x : 512 * x + 512])
        act = act[0:32] + act[32:64]
        gate = sigmoid(act)
        d_two[x] = gate * (1.0 + act * (1.0 - gate))
        value = act * gate
        total = value if x % 2 == 0 else total + value
        if x % 2 == 1:
            for my in range(2):
                cell = total[:, 256 * my : 256 * my + 128] + total[:, 256 * my + 128 : 256 * my + 256]
                cells.append((cell + pltpu.roll(cell, 126, 1)) * 0.125)
    quad = jnp.concatenate(cells, axis=1)
    row, col = iota((512, 128), 0), iota((512, 128), 1)
    pick = ((row >> 7) == (col >> 5)) & ((row & 127) == 4 * (col & 31))
    parts = mm(jnp.concatenate(split3(quad), axis=0), pick.astype(F32).astype(BF16))
    map_out[...] = xor_rows(parts[0:32] + parts[32:64] + parts[64:96], place[0], 2)

    row, col = iota((128, 512), 0), iota((128, 512), 1)
    pick = ((row >> 5) == (col >> 7)) & ((row & 31) == ((col & 127) >> 2)) & ((col & 1) == 0)
    parts = mm(jnp.concatenate(split3(up[...]), axis=0), pick.astype(F32).astype(BF16))
    wide = (parts[0:32] + parts[32:64] + parts[64:96]) * (0.125 * scale_up)
    highs, lows = [], []
    for x in range(4):
        for y in range(4):
            at = ((x // 2) * 2 + y // 2) * 128
            high, low = split2(wide[:, at : at + 128] * d_two[x, :, 128 * y : 128 * y + 128])
            highs.append(high)
            lows.append(low)
    high, low = jnp.concatenate(highs, axis=1), jnp.concatenate(lows, axis=1)
    grad_two = jnp.concatenate([high, low], axis=0)

    y_back[...] = mm(left_back[...], jnp.concatenate([grad_two, grad_two], axis=0))

    found = mm_nt(p_two[...], grad_two)
    found = found + pltpu.roll(jnp.concatenate([found, found], axis=1), 96, 1)[:, 0:64]
    groups = [found[32 * t : 32 * t + 16] + found[32 * t + 16 : 32 * t + 32] for t in range(27)]
    groups.append(found[864:880])
    slots = [jnp.concatenate(groups[7 * s : 7 * s + 7], axis=0)[:, 0:32] for s in range(4)]
    sums[0:112, :] = jnp.concatenate(slots, axis=1)

    for px in range(6):
        for py in range(6):
            acc = [None] * 3
            for a, b in TAPS:
                x, y = px - a, py - b
                if not (0 <= x < 4 and 0 <= y < 4):
                    continue
                at = (x * 4 + y) * 128
                for c in range(3):
                    start = ((a * 3 + b) * 3 + c) * 16
                    block = y_back[start : start + 16, at : at + 128]
                    acc[c] = block if acc[c] is None else acc[c] + block
            cell = acc[1] + lane_shift(acc[0], -2) + lane_shift(acc[2], 2)
            cell = (cell + pltpu.roll(cell, 1, 1)) * (0.125 * edge[px] * edge[6 + py])
            for dx in range(2):
                for dy in range(2):
                    x, y = 2 * px + dx, 2 * py + dy
                    high, low = split2(cell * d_one[x, :, 128 * y : 128 * y + 128])
                    at = (x * 12 + y) * 128
                    g_one[:, at : at + 128] = jnp.concatenate([high, low], axis=0)

    def last(step, total):
        at = pl.multiple_of(step * 3072, 3072)
        return total + mm_nt(p_one[:, pl.ds(at, 3072)], g_one[:, pl.ds(at, 3072)])

    found = lax.fori_loop(0, 6, last, jnp.zeros((224, 32), F32))
    found = (found[:, 0:16] + found[:, 16:32]).reshape(28, 8, 16)
    upper = jnp.concatenate([found[:, 4:8], found[:, 0:4]], axis=1)
    found = found + upper
    blank = jnp.zeros((8, 16), F32)
    blocks = [found[g] for g in range(28)] + [blank] * 4
    strips = [jnp.concatenate(blocks[8 * t : 8 * t + 8], axis=1) for t in range(4)]
    low_rows = iota((8, 128), 0) < 4
    sums[112:120, :] = jnp.where(low_rows, strips[0], strips[1])
    sums[120:128, :] = jnp.where(low_rows, strips[2], strips[3])


def finish(place, sums, other, mine, pooled, gk1, gb1, gk2, gb2):
    total = sums[...] + other[...]
    for g in range(27):
        s, t = g // 7, g % 7
        gk2[g] = total[16 * t : 16 * t + 16, 32 * s : 32 * s + 32]
    gb2[...] = total[96:97, 96:128]
    for g in range(27):
        t, s = g // 8, g % 8
        start = 112 + 8 * (t // 2) + 4 * (t % 2)
        gk1[g] = total[start : start + 4, 16 * s : 16 * s + 16]
    gb1[...] = total[124:125, 48:64]
    pooled[...] = xor_rows(mine[...], place[0], 2)


def shift_pairs(count, step):
    return [(i, i + step) for i in range(count) if 0 <= i + step < count]


def neighbours(block, axis, dim):
    count = lax.axis_size(axis)
    size = block.shape[dim]
    low = lax.slice_in_dim(block, size - HALO, size, axis=dim)
    high = lax.slice_in_dim(block, 0, HALO, axis=dim)
    return (
        lax.ppermute(low, axis, shift_pairs(count, 1)),
        lax.ppermute(high, axis, shift_pairs(count, -1)),
    )


def call(kernel, outs, ins, scratch=()):
    return pl.pallas_call(
        kernel,
        out_shape=[jax.ShapeDtypeStruct(*o) for o in outs],
        in_specs=[pl.BlockSpec(memory_space=m) for m in ins],
        out_specs=[pl.BlockSpec(memory_space=pltpu.VMEM) for _ in outs],
        scratch_shapes=list(scratch),
        compiler_params=VMEM,
    )


def on_device(volume, kernel_one, bias_one, kernel_two, bias_two, cotangent):
    gx, gy = lax.axis_index("gx"), lax.axis_index("gy")
    nx, ny = lax.axis_size("gx"), lax.axis_size("gy")
    vm, sm = pltpu.VMEM, pltpu.SMEM

    own = jnp.transpose(volume, (1, 2, 0, 3))
    xlo, xhi = neighbours(own, "gx", 0)
    full = jnp.concatenate([xlo, own, xhi], axis=0)
    ylo, yhi = neighbours(full, "gy", 1)

    send = jnp.transpose(cotangent.reshape(2, 2, 16, 64), (2, 0, 1, 3)).reshape(32, 128)
    up = lax.all_to_all(send, "gy", 0, 0, tiled=True)

    k1 = jnp.transpose(kernel_one, (2, 3, 4, 1, 0)).reshape(27, 4, 16)
    k2 = jnp.transpose(kernel_two, (2, 3, 4, 1, 0)).reshape(27, 16, 32)
    left_one, left_two, left_back = call(
        prepare, [((32, 224), BF16), ((64, 880), BF16), ((432, 128), BF16)], [vm] * 4
    )(k1, bias_one[None], k2, bias_two[None])

    inside = lambda at, size, n: jnp.where(
        ((at == 0) & (jnp.arange(6) == 0)) | ((at == n - 1) & (jnp.arange(6) == 5)), 0.0, 1.0
    )
    scale = 8.0 / (volume.shape[1] * nx)
    edge = jnp.concatenate(
        [inside(gx, 6, nx), inside(gy, 6, ny), jnp.full((4,), scale)]
    ).astype(F32)
    place = gy.astype(jnp.int32).reshape(1)

    mapped, sums = call(
        work,
        [((32, 128), F32), ((128, 128), F32)],
        [sm, sm] + [vm] * 9,
        [
            pltpu.VMEM((14, 14, 24, 128), F32),
            pltpu.VMEM((224, 18432), BF16),
            pltpu.VMEM((12, 16, 1536), F32),
            pltpu.VMEM((6, 6, 96, 128), BF16),
            pltpu.VMEM((880, 2048), BF16),
            pltpu.VMEM((4, 32, 512), F32),
            pltpu.VMEM((432, 2048), F32),
            pltpu.VMEM((32, 18432), BF16),
        ],
    )(place, edge, xlo, own, xhi, ylo, yhi, left_one, left_two, left_back, up)

    slots = mapped.reshape(2, 2, 2, 2, 2, 128)
    for bit in range(4):
        dim = 3 - bit
        kept, sent = (lax.index_in_dim(slots, k, dim, keepdims=True) for k in range(2))
        packed = jnp.concatenate([sums, sent.reshape(16, 128)], axis=0)
        got = lax.ppermute(packed, "gy", [(i, i ^ (1 << bit)) for i in range(16)])
        sums = sums + got[0:128]
        slots = jnp.concatenate([kept, got[128:144].reshape(sent.shape)], axis=dim)
    for bit in range(3):
        got = lax.ppermute(sums, "gx", [(i, i ^ (1 << bit)) for i in range(8)])
        if bit < 2:
            sums = sums + got

    pooled, gk1, gb1, gk2, gb2 = call(
        finish,
        [((32, 128), F32), ((27, 4, 16), F32), ((1, 16), F32), ((27, 16, 32), F32), ((1, 32), F32)],
        [sm] + [vm] * 3,
    )(place, sums, got, slots.reshape(32, 128))
    pooled = jnp.transpose(pooled.reshape(16, 2, 2, 64), (1, 2, 0, 3)).reshape(2, 2, 1024)
    gk1 = jnp.transpose(gk1.reshape(3, 3, 3, 4, 16), (4, 3, 0, 1, 2))
    gk2 = jnp.transpose(gk2.reshape(3, 3, 3, 16, 32), (4, 3, 0, 1, 2))
    return (pooled, gk1, gb1[0], gk2, gb2[0])


def solution(mesh):
    in_specs = (P(None, "gx", "gy", None), P(), P(), P(), P(), P("gy", "gx", None))
    out_specs = (P("gy", "gx", None), P(), P(), P(), P())
    return jax.shard_map(
        on_device, mesh=mesh, in_specs=in_specs, out_specs=out_specs, check_vma=False
    )
```

```python
import functools

import jax
import jax.numpy as jnp
from jax import lax
from jax.experimental import pallas as pl
from jax.experimental.pallas import tpu as pltpu
from jax.sharding import PartitionSpec as P

F32, BF16 = jnp.float32, jnp.bfloat16
HALO = 3
TAPS = [(a, b) for a in range(3) for b in range(3)]
NT = (((1,), (1,)), ((), ()))


def mm(left, right):
    return jnp.dot(left, right, preferred_element_type=F32)


def mm_nt(left, right):
    return lax.dot_general(left, right, NT, preferred_element_type=F32)


def split2(value):
    high = value.astype(BF16)
    return high, (value - high.astype(F32)).astype(BF16)


def split3(value):
    high, rest = split2(value)
    low = value - high.astype(F32) - rest.astype(F32)
    return high, rest, low.astype(BF16)


def iota(shape, dim):
    return lax.broadcasted_iota(jnp.int32, shape, dim)


def lane_shift(value, by):
    axis = value.ndim - 1
    lane = iota(value.shape, axis)
    moved = pltpu.roll(value, by % 128, axis)
    keep = lane >= by if by > 0 else lane < 128 + by
    return jnp.where(keep, moved, 0.0)


def sigmoid(value):
    return 1.0 / (1.0 + jnp.exp(-value))


def eye(size):
    return (iota((size, size), 0) == iota((size, size), 1)).astype(BF16)


def xor_rows(value, bits, rows_per):
    rows = value.shape[0]
    group = iota(value.shape, 0) // rows_per
    for bit in range(4):
        span = rows_per << bit
        upper = (group >> bit) & 1
        swapped = jnp.where(
            upper == 1,
            pltpu.roll(value, span, 0),
            pltpu.roll(value, rows - span, 0),
        )
        value = jnp.where(((bits >> bit) & 1) == 1, swapped, value)
    return value


def prepare(
    place, k1_hbm, b1_hbm, k2_hbm, b2_hbm, cot_hbm, left_one, left_two, left_back, send,
    k1, b1, k2, b2, cot, sems,
):
    moves = [
        pltpu.make_async_copy(source, target, sems.at[i])
        for i, (source, target) in enumerate(
            ((k1_hbm, k1), (b1_hbm, b1), (k2_hbm, k2), (b2_hbm, b2), (cot_hbm, cot))
        )
    ]
    for move in moves:
        move.start()
    for move in moves:
        move.wait()

    def ones_first(bias, rows):
        row = iota((rows, bias.shape[1]), 0)
        return jnp.where(row == 0, jnp.broadcast_to(bias, (rows, bias.shape[1])), 0.0)

    lower = iota((1, 128), 1) < 64
    rows = [None] * 32
    for f in range(2):
        for k in range(8):
            near, far = (cot[f, m : m + 1, 128 * k : 128 * k + 128] for m in range(2))
            rows[4 * k + f] = jnp.where(lower, near, pltpu.roll(far, 64, 1))
            rows[4 * k + 2 + f] = jnp.where(lower, pltpu.roll(near, 64, 1), far)
    send[...] = swap_last(xor_rows(jnp.concatenate(rows, axis=0), place[0], 2))

    taps = [jnp.concatenate([k1[t], k1[t]], axis=0) for t in range(27)]
    whole = jnp.concatenate(taps + [ones_first(b1[...], 8)], axis=0)
    high, low = split2(whole)
    left_one[0:16, :] = mm_nt(eye(16), high).astype(BF16)
    left_one[16:32, :] = mm_nt(eye(16), low).astype(BF16)
    taps = [jnp.concatenate([k2[t], k2[t]], axis=0) for t in range(27)]
    whole = jnp.concatenate(taps + [ones_first(b2[...], 16)], axis=0)
    high, low = split2(whole)
    left_two[0:32, :] = mm_nt(eye(32), high).astype(BF16)
    left_two[32:64, :] = mm_nt(eye(32), low).astype(BF16)
    for t in range(27):
        high, low = split2(k2[t])
        left_back[16 * t : 16 * t + 16, :] = jnp.concatenate([high, high, low, low], axis=1)


def columns(block):
    high = block.astype(BF16).astype(F32)
    both = jnp.concatenate([high, block - high], axis=1)
    return jnp.concatenate([lane_shift(both, 1), both, lane_shift(both, -1)], axis=1)


def forward(
    place, edge, xlo, own, xhi, ylo, yhi, left_one, left_two, unused,
    p_one, d_one, p_two, d_two, map_out,
    s_one, s_two,
):
    for ref, start in ((xlo, 0), (own, HALO), (xhi, HALO + own.shape[0])):
        for x in range(ref.shape[0]):
            s_one[start + x, 3:11] = columns(ref[x])
    for x in range(14):
        s_one[x, 0:3] = columns(ylo[x])
        s_one[x, 11:14] = columns(yhi[x])
    even = (iota((16, 128), 1) & 1) == 0
    one_row = (iota((8, 128), 0) == 0).astype(F32)

    for px in range(6):
        total = None
        for x in (2 * px, 2 * px + 1):
            at = 1536 * x
            for y in range(12):
                patch = jnp.concatenate([s_one[x + a, y + b] for a, b in TAPS] + [one_row], axis=0)
                p_one[:, at + 128 * y : at + 128 * y + 128] = patch.astype(BF16)
            act = mm(left_one[...], p_one[:, at : at + 1536])
            act = act[0:16] + act[16:32]
            gate = sigmoid(act)
            d_one[x] = gate * (1.0 + act * (1.0 - gate))
            total = act * gate if total is None else total + act * gate
        for py in range(6):
            at = 256 * py
            cell = total[:, at : at + 128] + total[:, at + 128 : at + 256]
            cell = cell + pltpu.roll(cell, 127, 1)
            cell = jnp.where(even, cell, 0.0) * (0.125 * edge[px] * edge[6 + py])
            for c, by in enumerate((2, 0, -2)):
                moved = lane_shift(cell, by) if by else cell
                high, low = split2(moved)
                s_two[px, py, 32 * c : 32 * c + 32, :] = jnp.concatenate([high, low], axis=0)

    ones_rows = (iota((16, 128), 0) == 0).astype(F32).astype(BF16)
    cells = []
    for x in range(4):
        for y in range(4):
            at = (x * 4 + y) * 128
            for t, (a, b) in enumerate(TAPS):
                p_two[96 * t : 96 * t + 96, at : at + 128] = s_two[x + a, y + b]
            p_two[864:880, at : at + 128] = ones_rows
        act = mm(left_two[...], p_two[:, 512 * x : 512 * x + 512])
        act = act[0:32] + act[32:64]
        gate = sigmoid(act)
        d_two[x] = gate * (1.0 + act * (1.0 - gate))
        value = act * gate
        total = value if x % 2 == 0 else total + value
        if x % 2 == 1:
            for my in range(2):
                cell = total[:, 256 * my : 256 * my + 128] + total[:, 256 * my + 128 : 256 * my + 256]
                cells.append((cell + pltpu.roll(cell, 126, 1)) * 0.125)
    quad = jnp.concatenate(cells, axis=1)
    row, col = iota((512, 128), 0), iota((512, 128), 1)
    pick = ((row >> 7) == (col >> 5)) & ((row & 127) == 4 * (col & 31))
    parts = mm(jnp.concatenate(split3(quad), axis=0), pick.astype(F32).astype(BF16))
    parts = parts[0:32] + parts[32:64] + parts[64:96]
    map_out[...] = swap_last(xor_rows(parts, place[0], 2))


def backward(
    place, edge, p_one, d_one, p_two, d_two, left_back, up, sums, y_back, g_one
):
    row, col = iota((128, 512), 0), iota((128, 512), 1)
    pick = ((row >> 5) == (col >> 7)) & ((row & 31) == ((col & 127) >> 2)) & ((col & 1) == 0)
    parts = mm(jnp.concatenate(split3(xor_rows(swap_last(up[...]), place[0], 2)), axis=0), pick.astype(F32).astype(BF16))
    wide = (parts[0:32] + parts[32:64] + parts[64:96]) * (0.125 * edge[12])
    highs, lows = [], []
    for x in range(4):
        for y in range(4):
            at = ((x // 2) * 2 + y // 2) * 128
            high, low = split2(wide[:, at : at + 128] * d_two[x, :, 128 * y : 128 * y + 128])
            highs.append(high)
            lows.append(low)
    high, low = jnp.concatenate(highs, axis=1), jnp.concatenate(lows, axis=1)
    grad_two = jnp.concatenate([high, low], axis=0)

    y_back[...] = mm(left_back[...], jnp.concatenate([grad_two, grad_two], axis=0))

    found = mm_nt(p_two[...], grad_two)
    found = found + pltpu.roll(jnp.concatenate([found, found], axis=1), 96, 1)[:, 0:64]
    groups = [found[32 * t : 32 * t + 16] + found[32 * t + 16 : 32 * t + 32] for t in range(27)]
    groups.append(found[864:880])
    slots = [jnp.concatenate(groups[7 * s : 7 * s + 7], axis=0)[:, 0:32] for s in range(4)]
    sums[0:112, :] = jnp.concatenate(slots, axis=1)

    for px in range(6):
        for py in range(6):
            acc = [None] * 3
            for a, b in TAPS:
                x, y = px - a, py - b
                if not (0 <= x < 4 and 0 <= y < 4):
                    continue
                at = (x * 4 + y) * 128
                for c in range(3):
                    start = ((a * 3 + b) * 3 + c) * 16
                    block = y_back[start : start + 16, at : at + 128]
                    acc[c] = block if acc[c] is None else acc[c] + block
            cell = acc[1] + lane_shift(acc[0], -2) + lane_shift(acc[2], 2)
            cell = (cell + pltpu.roll(cell, 1, 1)) * (0.125 * edge[px] * edge[6 + py])
            for dx in range(2):
                for dy in range(2):
                    x, y = 2 * px + dx, 2 * py + dy
                    high, low = split2(cell * d_one[x, :, 128 * y : 128 * y + 128])
                    at = (x * 12 + y) * 128
                    g_one[:, at : at + 128] = jnp.concatenate([high, low], axis=0)

    found = mm_nt(p_one[...], g_one[...])
    found = (found[:, 0:16] + found[:, 16:32]).reshape(28, 8, 16)
    upper = jnp.concatenate([found[:, 4:8], found[:, 0:4]], axis=1)
    found = found + upper
    blank = jnp.zeros((8, 16), F32)
    blocks = [found[g] for g in range(28)] + [blank] * 4
    strips = [jnp.concatenate(blocks[8 * t : 8 * t + 8], axis=1) for t in range(4)]
    low_rows = iota((8, 128), 0) < 4
    sums[112:120, :] = jnp.where(low_rows, strips[0], strips[1])
    sums[120:128, :] = jnp.where(low_rows, strips[2], strips[3])


def finish(place, mine, other, slots, pooled, gk1, gb1, gk2, gb2):
    total = mine[...] + other[...]
    for g in range(27):
        s, t = g // 7, g % 7
        gk2[g] = total[16 * t : 16 * t + 16, 32 * s : 32 * s + 32]
    gb2[...] = total[96:97, 96:128]
    for g in range(27):
        t, s = g // 8, g % 8
        start = 112 + 8 * (t // 2) + 4 * (t % 2)
        gk1[g] = total[start : start + 4, 16 * s : 16 * s + 16]
    gb1[...] = total[124:125, 48:64]
    value = xor_rows(swap_last(slots[...]), place[0], 2)
    turned = pltpu.roll(value, 64, 1)
    lower = iota((1, 128), 1) < 64
    for f in range(2):
        for k in range(8):
            at, near, far = slice(128 * k, 128 * k + 128), 4 * k + f, 4 * k + 2 + f
            pooled[f, 0:1, at] = jnp.where(lower, value[near : near + 1], turned[far : far + 1])
            pooled[f, 1:2, at] = jnp.where(lower, turned[near : near + 1], value[far : far + 1])


def neighbours(block, axis, dim, rider=None):
    count, size = lax.axis_size(axis), block.shape[dim]
    to_low = lax.slice_in_dim(block, 0, HALO, axis=dim)
    to_high = lax.slice_in_dim(block, size - HALO, size, axis=dim)
    odd = (lax.axis_index(axis) & 1) == 1

    def swap(start, value):
        pairs = [(i, i + 1) for i in range(start, count - 1, 2)]
        return lax.ppermute(value, axis, pairs + [(j, i) for i, j in pairs])

    inner = jnp.where(odd, to_low, to_high)
    if rider is None:
        inner, got = swap(0, inner), None
    else:
        rows = inner.size // 128
        both = swap(0, jnp.concatenate([inner.reshape(rows, 128), rider], axis=0))
        inner, got = both[:rows].reshape(inner.shape), both[rows:]
    outer = swap(1, jnp.where(odd, to_high, to_low))
    return jnp.where(odd, inner, outer), jnp.where(odd, outer, inner), got


def parts_of(slots, bit):
    shape = slots.shape[0] // (4 << bit), 2, (2 << bit), 128
    both = slots.reshape(shape)
    return both[:, 0], both[:, 1]


def joined(kept, got):
    return jnp.stack([kept, got.reshape(kept.shape)], axis=1).reshape(32, 128)


FLIPS = (1, 2, 4, 12)


def flip(value, axis, by):
    return lax.ppermute(value, axis, [(i, i ^ by) for i in range(lax.axis_size(axis))])


def regroup(slots, bit):
    kept, sent = parts_of(slots, bit)
    return joined(kept, flip(sent.reshape(16, 128), "gy", FLIPS[bit]))


def swap_last(value):
    return jnp.concatenate([value[0:16], value[24:32], value[16:24]], axis=0)


def call(kernel, outs, ins, scratch=(), cost=10**6):
    return pl.pallas_call(
        kernel,
        out_shape=[jax.ShapeDtypeStruct(*o) for o in outs],
        in_specs=[pl.BlockSpec(memory_space=m) for m in ins],
        out_specs=[pl.BlockSpec(memory_space=pltpu.VMEM) for _ in outs],
        scratch_shapes=[pltpu.VMEM(*s) if isinstance(s, tuple) else s for s in scratch],
        compiler_params=pltpu.CompilerParams(vmem_limit_bytes=24 * 2**20),
        cost_estimate=pl.CostEstimate(flops=cost, bytes_accessed=cost, transcendentals=0),
    )


def on_device(volume, kernel_one, bias_one, kernel_two, bias_two, cotangent):
    gx, gy = lax.axis_index("gx"), lax.axis_index("gy")
    nx, ny = lax.axis_size("gx"), lax.axis_size("gy")
    vm, sm = pltpu.VMEM, pltpu.SMEM

    place = gy.astype(jnp.int32).reshape(1)

    k1 = jnp.transpose(kernel_one, (2, 3, 4, 1, 0)).reshape(27, 4, 16)
    k2 = jnp.transpose(kernel_two, (2, 3, 4, 1, 0)).reshape(27, 16, 32)
    left_one, left_two, left_back, up = call(
        prepare,
        [((32, 224), BF16), ((64, 880), BF16), ((432, 128), BF16), ((32, 128), F32)],
        [sm] + [pltpu.HBM] * 5,
        [
            ((27, 4, 16), F32),
            ((1, 16), F32),
            ((27, 16, 32), F32),
            ((1, 32), F32),
            ((2, 2, 1024), F32),
            pltpu.SemaphoreType.DMA((5,)),
        ],
    )(place, *(pltpu.with_memory_space_constraint(v, pltpu.HBM) for v in (k1, bias_one[None], k2, bias_two[None], cotangent)))

    own = jnp.transpose(volume, (1, 2, 0, 3))
    xlo, xhi, _ = neighbours(own, "gx", 0)
    up = regroup(up, 3)
    full = jnp.concatenate([xlo, own, xhi], axis=0)
    kept, sent = parts_of(up, 0)
    ylo, yhi, got = neighbours(full, "gy", 1, sent.reshape(16, 128))
    ready = regroup(joined(kept, got), 2)
    up = regroup(ready, 1)

    inside = lambda at, size, n: jnp.where(
        ((at == 0) & (jnp.arange(6) == 0)) | ((at == n - 1) & (jnp.arange(6) == 5)), 0.0, 1.0
    )
    scale = 8.0 / (volume.shape[1] * nx)
    edge = jnp.concatenate(
        [inside(gx, 6, nx), inside(gy, 6, ny), jnp.full((4,), scale)]
    ).astype(F32)

    p_one, d_one, p_two, d_two, mapped = call(
        forward,
        [
            ((224, 18432), BF16),
            ((12, 16, 1536), F32),
            ((880, 2048), BF16),
            ((4, 32, 512), F32),
            ((32, 128), F32),
        ],
        [sm, sm] + [vm] * 7 + [pl.ANY],
        [((14, 14, 24, 128), F32), ((6, 6, 96, 128), BF16)],
        cost=10**7,
    )(place, edge, xlo, own, xhi, ylo, yhi, left_one, left_two, ready)
    (sums,) = call(
        backward,
        [((128, 128), F32)],
        [sm, sm] + [vm] * 6,
        [((432, 2048), F32), ((32, 18432), BF16)],
        cost=10**7,
    )(place, edge, p_one, d_one, p_two, d_two, left_back, up)

    slots = mapped
    for bit in range(4):
        kept, sent = parts_of(slots, bit)
        got = flip(jnp.concatenate([sums, sent.reshape(16, 128)], axis=0), "gy", FLIPS[bit])
        sums = sums + got[0:128]
        slots = joined(kept, got[128:144])
    sums = sums + flip(sums, "gx", 4)
    sums = sums + flip(sums, "gx", 1)
    other = flip(sums, "gx", 3)

    pooled, gk1, gb1, gk2, gb2 = call(
        finish,
        [((2, 2, 1024), F32), ((27, 4, 16), F32), ((1, 16), F32), ((27, 16, 32), F32), ((1, 32), F32)],
        [sm] + [vm] * 3,
    )(place, sums, other, slots)
    gk1 = jnp.transpose(gk1.reshape(3, 3, 3, 4, 16), (4, 3, 0, 1, 2))
    gk2 = jnp.transpose(gk2.reshape(3, 3, 3, 16, 32), (4, 3, 0, 1, 2))
    return (pooled, gk1, gb1[0], gk2, gb2[0])


def solution(mesh):
    in_specs = (P(None, "gx", "gy", None), P(), P(), P(), P(), P("gy", "gx", None))
    out_specs = (P("gy", "gx", None), P(), P(), P(), P())
    return jax.shard_map(
        on_device, mesh=mesh, in_specs=in_specs, out_specs=out_specs, check_vma=False
    )
```

```python
import functools

import jax
import jax.numpy as jnp
from jax import lax
from jax.experimental import pallas as pl
from jax.experimental.pallas import tpu as pltpu
from jax.sharding import PartitionSpec as P

F32, BF16 = jnp.float32, jnp.bfloat16
HALO = 3
TAPS = [(a, b) for a in range(3) for b in range(3)]
TAPS_ONE = [(a, b) for b in range(3) for a in range(3)]
NT = (((1,), (1,)), ((), ()))


def mm(left, right):
    return jnp.dot(left, right, preferred_element_type=F32)


def mm_nt(left, right):
    return lax.dot_general(left, right, NT, preferred_element_type=F32)


def split2(value):
    high = value.astype(BF16)
    return high, (value - high.astype(F32)).astype(BF16)


def split3(value):
    high, rest = split2(value)
    low = value - high.astype(F32) - rest.astype(F32)
    return high, rest, low.astype(BF16)


def iota(shape, dim):
    return lax.broadcasted_iota(jnp.int32, shape, dim)


def lane_shift(value, by):
    axis = value.ndim - 1
    lane = iota(value.shape, axis)
    moved = pltpu.roll(value, by % 128, axis)
    keep = lane >= by if by > 0 else lane < 128 + by
    return jnp.where(keep, moved, 0.0)


def sigmoid(value):
    return 1.0 / (1.0 + jnp.exp(-value))


def eye(size):
    return (iota((size, size), 0) == iota((size, size), 1)).astype(BF16)


def xor_rows(value, bits, rows_per):
    rows = value.shape[0]
    group = iota(value.shape, 0) // rows_per
    for bit in range(4):
        span = rows_per << bit
        upper = (group >> bit) & 1
        swapped = jnp.where(
            upper == 1,
            pltpu.roll(value, span, 0),
            pltpu.roll(value, rows - span, 0),
        )
        value = jnp.where(((bits >> bit) & 1) == 1, swapped, value)
    return value


def prepare(
    place, k1_hbm, b1_hbm, k2_hbm, b2_hbm, cot_hbm, left_one, left_two, left_back, send,
    k1, b1, k2, b2, cot, sems,
):
    moves = [
        pltpu.make_async_copy(source, target, sems.at[i])
        for i, (source, target) in enumerate(
            ((k1_hbm, k1), (b1_hbm, b1), (k2_hbm, k2), (b2_hbm, b2), (cot_hbm, cot))
        )
    ]
    for move in moves:
        move.start()
    for move in moves:
        move.wait()

    def ones_first(bias, rows):
        row = iota((rows, bias.shape[1]), 0)
        return jnp.where(row == 0, jnp.broadcast_to(bias, (rows, bias.shape[1])), 0.0)

    lower = iota((1, 128), 1) < 64
    rows = [None] * 32
    for f in range(2):
        for k in range(8):
            near, far = (cot[f, m : m + 1, 128 * k : 128 * k + 128] for m in range(2))
            rows[4 * k + f] = jnp.where(lower, near, pltpu.roll(far, 64, 1))
            rows[4 * k + 2 + f] = jnp.where(lower, pltpu.roll(near, 64, 1), far)
    send[...] = swap_last(xor_rows(jnp.concatenate(rows, axis=0), place[0], 2))

    order = [(a * 3 + b) * 3 + c for a, b in TAPS_ONE for c in range(3)]
    taps = [jnp.concatenate([k1[t], k1[t]], axis=0) for t in order]
    whole = jnp.concatenate(taps + [ones_first(b1[...], 8)], axis=0)
    high, low = split2(whole)
    left_one[0:16, :] = mm_nt(eye(16), high).astype(BF16)
    left_one[16:32, :] = mm_nt(eye(16), low).astype(BF16)
    taps = [jnp.concatenate([k2[t], k2[t]], axis=0) for t in range(27)]
    whole = jnp.concatenate(taps + [ones_first(b2[...], 16)], axis=0)
    high, low = split2(whole)
    left_two[0:32, :] = mm_nt(eye(32), high).astype(BF16)
    left_two[32:64, :] = mm_nt(eye(32), low).astype(BF16)
    for t in range(27):
        high, low = split2(k2[t])
        left_back[16 * t : 16 * t + 16, :] = jnp.concatenate([high, high, low, low], axis=1)


def columns(block):
    high = block.astype(BF16).astype(F32)
    both = jnp.concatenate([high, block - high], axis=1)
    return jnp.concatenate([lane_shift(both, 1), both, lane_shift(both, -1)], axis=1)


def forward_one(
    edge, xlo, own, xhi, ylo, yhi, left_one, unused, p_one, d_one, s_two, s_one
):
    for ref, start in ((xlo, 0), (own, HALO), (xhi, HALO + own.shape[0])):
        for x in range(ref.shape[0]):
            s_one[start + x, 3:11] = columns(ref[x])
    for x in range(14):
        s_one[x, 0:3] = columns(ylo[x])
        s_one[x, 11:14] = columns(yhi[x])
    even = (iota((16, 128), 1) & 1) == 0
    one_row = (iota((8, 128), 0) == 0).astype(F32)

    for px in range(6):
        total = None
        for x in (2 * px, 2 * px + 1):
            at = 1536 * x
            for y in range(12):
                patch = jnp.concatenate([s_one[x + a, y + b] for a, b in TAPS_ONE] + [one_row], axis=0)
                p_one[:, at + 128 * y : at + 128 * y + 128] = patch.astype(BF16)
            act = mm(left_one[...], p_one[:, at : at + 1536])
            act = act[0:16] + act[16:32]
            gate = sigmoid(act)
            d_one[x] = gate * (1.0 + act * (1.0 - gate))
            total = act * gate if total is None else total + act * gate
        for py in range(6):
            at = 256 * py
            cell = total[:, at : at + 128] + total[:, at + 128 : at + 256]
            cell = cell + pltpu.roll(cell, 127, 1)
            cell = jnp.where(even, cell, 0.0) * (0.125 * edge[px] * edge[6 + py])
            for c, by in enumerate((2, 0, -2)):
                moved = lane_shift(cell, by) if by else cell
                high, low = split2(moved)
                s_two[px, py, 32 * c : 32 * c + 32, :] = jnp.concatenate([high, low], axis=0)


def forward_two(place, s_two, left_two, unused, p_two, d_two, map_out):
    ones_rows = (iota((16, 128), 0) == 0).astype(F32).astype(BF16)
    cells = []
    for x in range(4):
        for y in range(4):
            at = (x * 4 + y) * 128
            for t, (a, b) in enumerate(TAPS):
                p_two[96 * t : 96 * t + 96, at : at + 128] = s_two[x + a, y + b]
            p_two[864:880, at : at + 128] = ones_rows
        act = mm(left_two[...], p_two[:, 512 * x : 512 * x + 512])
        act = act[0:32] + act[32:64]
        gate = sigmoid(act)
        d_two[x] = gate * (1.0 + act * (1.0 - gate))
        value = act * gate
        total = value if x % 2 == 0 else total + value
        if x % 2 == 1:
            for my in range(2):
                cell = total[:, 256 * my : 256 * my + 128] + total[:, 256 * my + 128 : 256 * my + 256]
                cells.append((cell + pltpu.roll(cell, 126, 1)) * 0.125)
    quad = jnp.concatenate(cells, axis=1)
    row, col = iota((512, 128), 0), iota((512, 128), 1)
    pick = ((row >> 7) == (col >> 5)) & ((row & 127) == 4 * (col & 31))
    parts = mm(jnp.concatenate(split3(quad), axis=0), pick.astype(F32).astype(BF16))
    parts = parts[0:32] + parts[32:64] + parts[64:96]
    map_out[...] = swap_last(xor_rows(parts, place[0], 2))


def backward(
    place, edge, p_one, d_one, p_two, d_two, left_back, up, sums, y_back, g_one
):
    row, col = iota((128, 512), 0), iota((128, 512), 1)
    pick = ((row >> 5) == (col >> 7)) & ((row & 31) == ((col & 127) >> 2)) & ((col & 1) == 0)
    parts = mm(jnp.concatenate(split3(xor_rows(swap_last(up[...]), place[0], 2)), axis=0), pick.astype(F32).astype(BF16))
    wide = (parts[0:32] + parts[32:64] + parts[64:96]) * (0.125 * edge[12])
    highs, lows = [], []
    for x in range(4):
        for y in range(4):
            at = ((x // 2) * 2 + y // 2) * 128
            high, low = split2(wide[:, at : at + 128] * d_two[x, :, 128 * y : 128 * y + 128])
            highs.append(high)
            lows.append(low)
    high, low = jnp.concatenate(highs, axis=1), jnp.concatenate(lows, axis=1)
    grad_two = jnp.concatenate([high, low], axis=0)

    y_back[...] = mm(left_back[...], jnp.concatenate([grad_two, grad_two], axis=0))

    found = mm_nt(p_two[...], grad_two)
    found = found + pltpu.roll(jnp.concatenate([found, found], axis=1), 96, 1)[:, 0:64]
    groups = [found[32 * t : 32 * t + 16] + found[32 * t + 16 : 32 * t + 32] for t in range(27)]
    groups.append(found[864:880])
    slots = [jnp.concatenate(groups[7 * s : 7 * s + 7], axis=0)[:, 0:32] for s in range(4)]
    sums[0:112, :] = jnp.concatenate(slots, axis=1)

    blank = jnp.zeros((32, 128), F32).astype(BF16)
    whole = jnp.zeros((16, 128), F32)
    found = jnp.zeros((80, 96), F32)
    for px in range(6):
        for x in (2 * px, 2 * px + 1):
            for b, y in ((0, 12), (0, 13), (1, 0), (1, 13), (2, 0), (2, 1)):
                at = (x * 14 + y) * 128
                g_one[32 * b : 32 * b + 32, at : at + 128] = blank
        for py in range(6):
            acc = [None] * 3
            for a, b in TAPS:
                x, y = px - a, py - b
                if not (0 <= x < 4 and 0 <= y < 4):
                    continue
                at = (x * 4 + y) * 128
                for c in range(3):
                    start = ((a * 3 + b) * 3 + c) * 16
                    block = y_back[start : start + 16, at : at + 128]
                    acc[c] = block if acc[c] is None else acc[c] + block
            cell = acc[1] + lane_shift(acc[0], -2) + lane_shift(acc[2], 2)
            cell = (cell + pltpu.roll(cell, 1, 1)) * (0.125 * edge[px] * edge[6 + py])
            for dx in range(2):
                for dy in range(2):
                    x, y = 2 * px + dx, 2 * py + dy
                    grad = cell * d_one[x, :, 128 * y : 128 * y + 128]
                    whole = whole + grad
                    both = jnp.concatenate(split2(grad), axis=0)
                    for b in range(3):
                        at = (x * 14 + y + b) * 128
                        g_one[32 * b : 32 * b + 32, at : at + 128] = both
        for x in (2 * px, 2 * px + 1):
            at, to = 1536 * x, 1792 * x
            found = found + mm_nt(p_one[0:80, at : at + 1536], g_one[:, to : to + 1536])
            found = found + mm_nt(p_one[144:224, at + 1280 : at + 1536], g_one[:, to + 1536 : to + 1792])

    by_b = [found[:, 32 * b : 32 * b + 16] + found[:, 32 * b + 16 : 32 * b + 32] for b in range(3)]
    groups = [by_b[b][(a * 3 + c) * 8 : (a * 3 + c) * 8 + 8] for a, b in TAPS for c in range(3)]
    ones = (iota((8, 128), 0) == 0).astype(F32).astype(BF16)
    groups.append(sum(mm_nt(ones, part) for part in split3(whole)))
    found = jnp.concatenate(groups, axis=0).reshape(28, 8, 16)
    found = found + jnp.concatenate([found[:, 4:8], found[:, 0:4]], axis=1)
    blank = jnp.zeros((8, 16), F32)
    blocks = [found[g] for g in range(28)] + [blank] * 4
    strips = [jnp.concatenate(blocks[8 * t : 8 * t + 8], axis=1) for t in range(4)]
    low_rows = iota((8, 128), 0) < 4
    sums[112:120, :] = jnp.where(low_rows, strips[0], strips[1])
    sums[120:128, :] = jnp.where(low_rows, strips[2], strips[3])


def finish(place, mine, other, slots, pooled, gk1, gb1, gk2, gb2):
    total = mine[...] + other[...]
    for g in range(27):
        s, t = g // 7, g % 7
        gk2[g] = total[16 * t : 16 * t + 16, 32 * s : 32 * s + 32]
    gb2[...] = total[96:97, 96:128]
    for g in range(27):
        t, s = g // 8, g % 8
        start = 112 + 8 * (t // 2) + 4 * (t % 2)
        gk1[g] = total[start : start + 4, 16 * s : 16 * s + 16]
    gb1[...] = total[124:125, 48:64]
    value = xor_rows(swap_last(slots[...]), place[0], 2)
    turned = pltpu.roll(value, 64, 1)
    lower = iota((1, 128), 1) < 64
    for f in range(2):
        for k in range(8):
            at, near, far = slice(128 * k, 128 * k + 128), 4 * k + f, 4 * k + 2 + f
            pooled[f, 0:1, at] = jnp.where(lower, value[near : near + 1], turned[far : far + 1])
            pooled[f, 1:2, at] = jnp.where(lower, turned[near : near + 1], value[far : far + 1])


def neighbours(block, axis, dim):
    count, size = lax.axis_size(axis), block.shape[dim]
    to_low = lax.slice_in_dim(block, 0, HALO, axis=dim)
    to_high = lax.slice_in_dim(block, size - HALO, size, axis=dim)
    odd = (lax.axis_index(axis) & 1) == 1

    def swap(start, value):
        pairs = [(i, i + 1) for i in range(start, count - 1, 2)]
        return lax.ppermute(value, axis, pairs + [(j, i) for i, j in pairs])

    inner = swap(0, jnp.where(odd, to_low, to_high))
    outer = swap(1, jnp.where(odd, to_high, to_low))
    return jnp.where(odd, inner, outer), jnp.where(odd, outer, inner), inner


def parts_of(slots, bit):
    shape = slots.shape[0] // (4 << bit), 2, (2 << bit), 128
    both = slots.reshape(shape)
    return both[:, 0], both[:, 1]


def joined(kept, got):
    return jnp.stack([kept, got.reshape(kept.shape)], axis=1).reshape(32, 128)


FLIPS = (1, 2, 4, 12)


def flip(value, axis, by):
    return lax.ppermute(value, axis, [(i, i ^ by) for i in range(lax.axis_size(axis))])


def regroup(slots, bit):
    kept, sent = parts_of(slots, bit)
    return joined(kept, flip(sent.reshape(16, 128), "gy", FLIPS[bit]))


def after(rows, other):
    return rows + 0.0 * other[(0,) * (other.ndim - 1)][None]


def swap_last(value):
    return jnp.concatenate([value[0:16], value[24:32], value[16:24]], axis=0)


def call(kernel, outs, ins, scratch=(), cost=10**6):
    return pl.pallas_call(
        kernel,
        out_shape=[jax.ShapeDtypeStruct(*o) for o in outs],
        in_specs=[pl.BlockSpec(memory_space=m) for m in ins],
        out_specs=[pl.BlockSpec(memory_space=pltpu.VMEM) for _ in outs],
        scratch_shapes=[pltpu.VMEM(*s) if isinstance(s, tuple) else s for s in scratch],
        compiler_params=pltpu.CompilerParams(vmem_limit_bytes=24 * 2**20),
        cost_estimate=pl.CostEstimate(flops=cost, bytes_accessed=cost, transcendentals=0),
    )


def on_device(volume, kernel_one, bias_one, kernel_two, bias_two, cotangent):
    gx, gy = lax.axis_index("gx"), lax.axis_index("gy")
    nx, ny = lax.axis_size("gx"), lax.axis_size("gy")
    vm, sm = pltpu.VMEM, pltpu.SMEM

    place = gy.astype(jnp.int32).reshape(1)

    k1 = jnp.transpose(kernel_one, (2, 3, 4, 1, 0)).reshape(27, 4, 16)
    k2 = jnp.transpose(kernel_two, (2, 3, 4, 1, 0)).reshape(27, 16, 32)
    left_one, left_two, left_back, up = call(
        prepare,
        [((32, 224), BF16), ((64, 880), BF16), ((432, 128), BF16), ((32, 128), F32)],
        [sm] + [pltpu.HBM] * 5,
        [
            ((27, 4, 16), F32),
            ((1, 16), F32),
            ((27, 16, 32), F32),
            ((1, 32), F32),
            ((2, 2, 1024), F32),
            pltpu.SemaphoreType.DMA((5,)),
        ],
    )(place, *(pltpu.with_memory_space_constraint(v, pltpu.HBM) for v in (k1, bias_one[None], k2, bias_two[None], cotangent)))

    own = jnp.transpose(volume, (1, 2, 0, 3))
    xlo, xhi, _ = neighbours(own, "gx", 0)
    full = jnp.concatenate([xlo, own, xhi], axis=0)
    ylo, yhi, inner = neighbours(full, "gy", 1)
    turn_one = regroup(up, 3)
    turn_two = regroup(after(turn_one, inner), 2)
    turn_three = regroup(turn_two, 1)
    up = regroup(turn_three, 0)

    inside = lambda at, size, n: jnp.where(
        ((at == 0) & (jnp.arange(6) == 0)) | ((at == n - 1) & (jnp.arange(6) == 5)), 0.0, 1.0
    )
    scale = 8.0 / (volume.shape[1] * nx)
    edge = jnp.concatenate(
        [inside(gx, 6, nx), inside(gy, 6, ny), jnp.full((4,), scale)]
    ).astype(F32)

    p_one, d_one, s_two = call(
        forward_one,
        [((224, 18432), BF16), ((12, 16, 1536), F32), ((6, 6, 96, 128), BF16)],
        [sm] + [vm] * 6 + [pl.ANY],
        [((14, 14, 24, 128), F32)],
        cost=10**7,
    )(edge, xlo, own, xhi, ylo, yhi, left_one, turn_two)
    p_two, d_two, mapped = call(
        forward_two,
        [((880, 2048), BF16), ((4, 32, 512), F32), ((32, 128), F32)],
        [sm] + [vm] * 2 + [pl.ANY],
        cost=10**7,
    )(place, s_two, left_two, turn_three)
    (sums,) = call(
        backward,
        [((128, 128), F32)],
        [sm, sm] + [vm] * 6,
        [((432, 2048), F32), ((96, 21504), BF16)],
        cost=10**7,
    )(place, edge, p_one, d_one, p_two, d_two, left_back, up)

    slots = mapped
    for bit in range(4):
        kept, sent = parts_of(slots, bit)
        got = flip(jnp.concatenate([sums, sent.reshape(16, 128)], axis=0), "gy", FLIPS[bit])
        sums = sums + got[0:128]
        slots = joined(kept, got[128:144])
    sums = sums + flip(sums, "gx", 4)
    sums = sums + flip(sums, "gx", 1)
    other = flip(sums, "gx", 3)

    pooled, gk1, gb1, gk2, gb2 = call(
        finish,
        [((2, 2, 1024), F32), ((27, 4, 16), F32), ((1, 16), F32), ((27, 16, 32), F32), ((1, 32), F32)],
        [sm] + [vm] * 3,
    )(place, sums, other, slots)
    gk1 = jnp.transpose(gk1.reshape(3, 3, 3, 4, 16), (4, 3, 0, 1, 2))
    gk2 = jnp.transpose(gk2.reshape(3, 3, 3, 16, 32), (4, 3, 0, 1, 2))
    return (pooled, gk1, gb1[0], gk2, gb2[0])


def solution(mesh):
    in_specs = (P(None, "gx", "gy", None), P(), P(), P(), P(), P("gy", "gx", None))
    out_specs = (P("gy", "gx", None), P(), P(), P(), P())
    return jax.shard_map(
        on_device, mesh=mesh, in_specs=in_specs, out_specs=out_specs, check_vma=False
    )
```

```python
import functools

import jax
import jax.numpy as jnp
from jax import lax
from jax.experimental import pallas as pl
from jax.experimental.pallas import tpu as pltpu
from jax.sharding import PartitionSpec as P

F32, BF16 = jnp.float32, jnp.bfloat16
HALO = 3
TAPS = [(a, b) for a in range(3) for b in range(3)]
TAPS_ONE = [(a, b) for b in range(3) for a in range(3)]
NT = (((1,), (1,)), ((), ()))


def mm(left, right):
    return jnp.dot(left, right, preferred_element_type=F32)


def mm_nt(left, right):
    return lax.dot_general(left, right, NT, preferred_element_type=F32)


def split2(value):
    high = value.astype(BF16)
    return high, (value - high.astype(F32)).astype(BF16)


def split3(value):
    high, rest = split2(value)
    low = value - high.astype(F32) - rest.astype(F32)
    return high, rest, low.astype(BF16)


def iota(shape, dim):
    return lax.broadcasted_iota(jnp.int32, shape, dim)


def lane_shift(value, by):
    axis = value.ndim - 1
    lane = iota(value.shape, axis)
    moved = pltpu.roll(value, by % 128, axis)
    keep = lane >= by if by > 0 else lane < 128 + by
    return jnp.where(keep, moved, 0.0)


def sigmoid(value):
    return 1.0 / (1.0 + jnp.exp(-value))


def eye(size):
    return (iota((size, size), 0) == iota((size, size), 1)).astype(BF16)


def xor_rows(value, bits, rows_per):
    rows = value.shape[0]
    group = iota(value.shape, 0) // rows_per
    for bit in range(4):
        span = rows_per << bit
        upper = (group >> bit) & 1
        swapped = jnp.where(
            upper == 1,
            pltpu.roll(value, span, 0),
            pltpu.roll(value, rows - span, 0),
        )
        value = jnp.where(((bits >> bit) & 1) == 1, swapped, value)
    return value


def fetch(pairs, sems):
    moves = [pltpu.make_async_copy(*pair, sems.at[i]) for i, pair in enumerate(pairs)]
    for move in moves:
        move.start()
    for move in moves:
        move.wait()


def arrange(place, cot_hbm, send, cot, sems):
    fetch([(cot_hbm, cot)], sems)
    lower = iota((1, 128), 1) < 64
    rows = [None] * 32
    for f in range(2):
        for k in range(8):
            near, far = (cot[f, m : m + 1, 128 * k : 128 * k + 128] for m in range(2))
            rows[4 * k + f] = jnp.where(lower, near, pltpu.roll(far, 64, 1))
            rows[4 * k + 2 + f] = jnp.where(lower, pltpu.roll(near, 64, 1), far)
    send[...] = swap_last(xor_rows(jnp.concatenate(rows, axis=0), place[0], 2))


def prepare(
    k1_hbm, b1_hbm, k2_hbm, b2_hbm, slots, left_one, left_two, left_back, passed, k1, b1, k2, b2, sems
):
    passed[...] = slots[...]
    fetch([(k1_hbm, k1), (b1_hbm, b1), (k2_hbm, k2), (b2_hbm, b2)], sems)

    def ones_first(bias, rows):
        row = iota((rows, bias.shape[1]), 0)
        return jnp.where(row == 0, jnp.broadcast_to(bias, (rows, bias.shape[1])), 0.0)

    order = [(a * 3 + b) * 3 + c for a, b in TAPS_ONE for c in range(3)]
    taps = [jnp.concatenate([k1[t], k1[t]], axis=0) for t in order]
    whole = jnp.concatenate(taps + [ones_first(b1[...], 8)], axis=0)
    high, low = split2(whole)
    left_one[0:16, :] = mm_nt(eye(16), high).astype(BF16)
    left_one[16:32, :] = mm_nt(eye(16), low).astype(BF16)
    taps = [jnp.concatenate([k2[t], k2[t]], axis=0) for t in range(27)]
    whole = jnp.concatenate(taps + [ones_first(b2[...], 16)], axis=0)
    high, low = split2(whole)
    left_two[0:32, :] = mm_nt(eye(32), high).astype(BF16)
    left_two[32:64, :] = mm_nt(eye(32), low).astype(BF16)
    for t in range(27):
        high, low = split2(k2[t])
        left_back[16 * t : 16 * t + 16, :] = jnp.concatenate([high, high, low, low], axis=1)


def columns(block):
    high = block.astype(BF16).astype(F32)
    both = jnp.concatenate([high, block - high], axis=1)
    return jnp.concatenate([lane_shift(both, 1), both, lane_shift(both, -1)], axis=1)


def forward_one(
    edge, xlo, own, xhi, ylo, yhi, left_one, unused, p_one, d_one, s_two, s_one
):
    for ref, start in ((xlo, 0), (own, HALO), (xhi, HALO + own.shape[0])):
        for x in range(ref.shape[0]):
            s_one[start + x, 3:11] = columns(ref[x])
    for x in range(14):
        s_one[x, 0:3] = columns(ylo[x])
        s_one[x, 11:14] = columns(yhi[x])
    even = (iota((16, 128), 1) & 1) == 0
    one_row = (iota((8, 128), 0) == 0).astype(F32)

    for px in range(6):
        total = None
        for x in (2 * px, 2 * px + 1):
            at = 1536 * x
            for y in range(12):
                patch = jnp.concatenate([s_one[x + a, y + b] for a, b in TAPS_ONE] + [one_row], axis=0)
                p_one[:, at + 128 * y : at + 128 * y + 128] = patch.astype(BF16)
            act = mm(left_one[...], p_one[:, at : at + 1536])
            act = act[0:16] + act[16:32]
            gate = sigmoid(act)
            d_one[x] = gate * (1.0 + act * (1.0 - gate))
            total = act * gate if total is None else total + act * gate
        for py in range(6):
            at = 256 * py
            cell = total[:, at : at + 128] + total[:, at + 128 : at + 256]
            cell = cell + pltpu.roll(cell, 127, 1)
            cell = jnp.where(even, cell, 0.0) * (0.125 * edge[px] * edge[6 + py])
            for c, by in enumerate((2, 0, -2)):
                moved = lane_shift(cell, by) if by else cell
                high, low = split2(moved)
                s_two[px, py, 32 * c : 32 * c + 32, :] = jnp.concatenate([high, low], axis=0)


def forward_two(place, s_two, left_two, unused, p_two, d_two, map_out):
    ones_rows = (iota((16, 128), 0) == 0).astype(F32).astype(BF16)
    cells = []
    for x in range(4):
        for y in range(4):
            at = (x * 4 + y) * 128
            for t, (a, b) in enumerate(TAPS):
                p_two[96 * t : 96 * t + 96, at : at + 128] = s_two[x + a, y + b]
            p_two[864:880, at : at + 128] = ones_rows
        act = mm(left_two[...], p_two[:, 512 * x : 512 * x + 512])
        act = act[0:32] + act[32:64]
        gate = sigmoid(act)
        d_two[x] = gate * (1.0 + act * (1.0 - gate))
        value = act * gate
        total = value if x % 2 == 0 else total + value
        if x % 2 == 1:
            for my in range(2):
                cell = total[:, 256 * my : 256 * my + 128] + total[:, 256 * my + 128 : 256 * my + 256]
                cells.append((cell + pltpu.roll(cell, 126, 1)) * 0.125)
    quad = jnp.concatenate(cells, axis=1)
    row, col = iota((512, 128), 0), iota((512, 128), 1)
    pick = ((row >> 7) == (col >> 5)) & ((row & 127) == 4 * (col & 31))
    parts = mm(jnp.concatenate(split3(quad), axis=0), pick.astype(F32).astype(BF16))
    parts = parts[0:32] + parts[32:64] + parts[64:96]
    map_out[...] = swap_last(xor_rows(parts, place[0], 2))


def backward(
    place, edge, p_one, d_one, p_two, d_two, left_back, up, sums, y_back, g_one
):
    row, col = iota((128, 512), 0), iota((128, 512), 1)
    pick = ((row >> 5) == (col >> 7)) & ((row & 31) == ((col & 127) >> 2)) & ((col & 1) == 0)
    parts = mm(jnp.concatenate(split3(xor_rows(swap_last(up[...]), place[0], 2)), axis=0), pick.astype(F32).astype(BF16))
    wide = (parts[0:32] + parts[32:64] + parts[64:96]) * (0.125 * edge[12])
    highs, lows = [], []
    for x in range(4):
        for y in range(4):
            at = ((x // 2) * 2 + y // 2) * 128
            high, low = split2(wide[:, at : at + 128] * d_two[x, :, 128 * y : 128 * y + 128])
            highs.append(high)
            lows.append(low)
    high, low = jnp.concatenate(highs, axis=1), jnp.concatenate(lows, axis=1)
    grad_two = jnp.concatenate([high, low], axis=0)

    y_back[...] = mm(left_back[...], jnp.concatenate([grad_two, grad_two], axis=0))

    found = mm_nt(p_two[...], grad_two)
    found = found + pltpu.roll(jnp.concatenate([found, found], axis=1), 96, 1)[:, 0:64]
    groups = [found[32 * t : 32 * t + 16] + found[32 * t + 16 : 32 * t + 32] for t in range(27)]
    groups.append(found[864:880])
    slots = [jnp.concatenate(groups[7 * s : 7 * s + 7], axis=0)[:, 0:32] for s in range(4)]
    sums[0:112, :] = jnp.concatenate(slots, axis=1)

    blank = jnp.zeros((32, 128), F32).astype(BF16)
    whole = jnp.zeros((16, 128), F32)
    found = jnp.zeros((80, 96), F32)
    for px in range(6):
        for x in (2 * px, 2 * px + 1):
            for b, y in ((0, 12), (0, 13), (1, 0), (1, 13), (2, 0), (2, 1)):
                at = (x * 14 + y) * 128
                g_one[32 * b : 32 * b + 32, at : at + 128] = blank
        for py in range(6):
            acc = [None] * 3
            for a, b in TAPS:
                x, y = px - a, py - b
                if not (0 <= x < 4 and 0 <= y < 4):
                    continue
                at = (x * 4 + y) * 128
                for c in range(3):
                    start = ((a * 3 + b) * 3 + c) * 16
                    block = y_back[start : start + 16, at : at + 128]
                    acc[c] = block if acc[c] is None else acc[c] + block
            cell = acc[1] + lane_shift(acc[0], -2) + lane_shift(acc[2], 2)
            cell = (cell + pltpu.roll(cell, 1, 1)) * (0.125 * edge[px] * edge[6 + py])
            for dx in range(2):
                for dy in range(2):
                    x, y = 2 * px + dx, 2 * py + dy
                    grad = cell * d_one[x, :, 128 * y : 128 * y + 128]
                    whole = whole + grad
                    both = jnp.concatenate(split2(grad), axis=0)
                    for b in range(3):
                        at = (x * 14 + y + b) * 128
                        g_one[32 * b : 32 * b + 32, at : at + 128] = both
        for x in (2 * px, 2 * px + 1):
            at, to = 1536 * x, 1792 * x
            found = found + mm_nt(p_one[0:80, at : at + 1536], g_one[:, to : to + 1536])
            found = found + mm_nt(p_one[144:224, at + 1280 : at + 1536], g_one[:, to + 1536 : to + 1792])

    by_b = [found[:, 32 * b : 32 * b + 16] + found[:, 32 * b + 16 : 32 * b + 32] for b in range(3)]
    groups = [by_b[b][(a * 3 + c) * 8 : (a * 3 + c) * 8 + 8] for a, b in TAPS for c in range(3)]
    ones = (iota((8, 128), 0) == 0).astype(F32).astype(BF16)
    groups.append(sum(mm_nt(ones, part) for part in split3(whole)))
    found = jnp.concatenate(groups, axis=0).reshape(28, 8, 16)
    found = found + jnp.concatenate([found[:, 4:8], found[:, 0:4]], axis=1)
    blank = jnp.zeros((8, 16), F32)
    blocks = [found[g] for g in range(28)] + [blank] * 4
    strips = [jnp.concatenate(blocks[8 * t : 8 * t + 8], axis=1) for t in range(4)]
    low_rows = iota((8, 128), 0) < 4
    sums[112:120, :] = jnp.where(low_rows, strips[0], strips[1])
    sums[120:128, :] = jnp.where(low_rows, strips[2], strips[3])


def finish(place, mine, other, slots, pooled, gk1, gb1, gk2, gb2):
    total = mine[...] + other[...]
    for g in range(27):
        s, t = g // 7, g % 7
        gk2[g] = total[16 * t : 16 * t + 16, 32 * s : 32 * s + 32]
    gb2[...] = total[96:97, 96:128]
    for g in range(27):
        t, s = g // 8, g % 8
        start = 112 + 8 * (t // 2) + 4 * (t % 2)
        gk1[g] = total[start : start + 4, 16 * s : 16 * s + 16]
    gb1[...] = total[124:125, 48:64]
    value = xor_rows(swap_last(slots[...]), place[0], 2)
    turned = pltpu.roll(value, 64, 1)
    lower = iota((1, 128), 1) < 64
    for f in range(2):
        for k in range(8):
            at, near, far = slice(128 * k, 128 * k + 128), 4 * k + f, 4 * k + 2 + f
            pooled[f, 0:1, at] = jnp.where(lower, value[near : near + 1], turned[far : far + 1])
            pooled[f, 1:2, at] = jnp.where(lower, turned[near : near + 1], value[far : far + 1])


def neighbours(block, axis, dim):
    count, size = lax.axis_size(axis), block.shape[dim]
    to_low = lax.slice_in_dim(block, 0, HALO, axis=dim)
    to_high = lax.slice_in_dim(block, size - HALO, size, axis=dim)
    odd = (lax.axis_index(axis) & 1) == 1

    def swap(start, value):
        pairs = [(i, i + 1) for i in range(start, count - 1, 2)]
        return lax.ppermute(value, axis, pairs + [(j, i) for i, j in pairs])

    inner = swap(0, jnp.where(odd, to_low, to_high))
    outer = swap(1, jnp.where(odd, to_high, to_low))
    return jnp.where(odd, inner, outer), jnp.where(odd, outer, inner), inner


def parts_of(slots, bit):
    shape = slots.shape[0] // (4 << bit), 2, (2 << bit), 128
    both = slots.reshape(shape)
    return both[:, 0], both[:, 1]


def joined(kept, got):
    return jnp.stack([kept, got.reshape(kept.shape)], axis=1).reshape(32, 128)


FLIPS = (1, 2, 4, 12)


def flip(value, axis, by):
    return lax.ppermute(value, axis, [(i, i ^ by) for i in range(lax.axis_size(axis))])


def regroup(slots, bit):
    kept, sent = parts_of(slots, bit)
    return joined(kept, flip(sent.reshape(16, 128), "gy", FLIPS[bit]))


def after(rows, other):
    return rows + 0.0 * other[(0,) * (other.ndim - 1)][None]


def swap_last(value):
    return jnp.concatenate([value[0:16], value[24:32], value[16:24]], axis=0)


def call(kernel, outs, ins, scratch=(), cost=10**6):
    return pl.pallas_call(
        kernel,
        out_shape=[jax.ShapeDtypeStruct(*o) for o in outs],
        in_specs=[pl.BlockSpec(memory_space=m) for m in ins],
        out_specs=[pl.BlockSpec(memory_space=pltpu.VMEM) for _ in outs],
        scratch_shapes=[pltpu.VMEM(*s) if isinstance(s, tuple) else s for s in scratch],
        compiler_params=pltpu.CompilerParams(vmem_limit_bytes=24 * 2**20),
        cost_estimate=pl.CostEstimate(flops=cost, bytes_accessed=cost, transcendentals=0),
    )


def on_device(volume, kernel_one, bias_one, kernel_two, bias_two, cotangent):
    gx, gy = lax.axis_index("gx"), lax.axis_index("gy")
    nx, ny = lax.axis_size("gx"), lax.axis_size("gy")
    vm, sm = pltpu.VMEM, pltpu.SMEM

    place = gy.astype(jnp.int32).reshape(1)

    k1 = jnp.transpose(kernel_one, (2, 3, 4, 1, 0)).reshape(27, 4, 16)
    k2 = jnp.transpose(kernel_two, (2, 3, 4, 1, 0)).reshape(27, 16, 32)
    in_hbm = lambda *values: [pltpu.with_memory_space_constraint(v, pltpu.HBM) for v in values]
    (up,) = call(
        arrange,
        [((32, 128), F32)],
        [sm, pltpu.HBM],
        [((2, 2, 1024), F32), pltpu.SemaphoreType.DMA((1,))],
    )(place, *in_hbm(cotangent))

    own = jnp.transpose(volume, (1, 2, 0, 3))
    xlo, xhi, _ = neighbours(own, "gx", 0)
    full = jnp.concatenate([xlo, own, xhi], axis=0)
    ylo, yhi, inner = neighbours(full, "gy", 1)
    turn_one = regroup(up, 3)
    turn_two = regroup(after(turn_one, inner), 2)
    left_one, left_two, left_back, passed = call(
        prepare,
        [((32, 224), BF16), ((64, 880), BF16), ((432, 128), BF16), ((32, 128), F32)],
        [pltpu.HBM] * 4 + [vm],
        [
            ((27, 4, 16), F32),
            ((1, 16), F32),
            ((27, 16, 32), F32),
            ((1, 32), F32),
            pltpu.SemaphoreType.DMA((4,)),
        ],
    )(*in_hbm(k1, bias_one[None], k2, bias_two[None]), turn_two)
    turn_three = regroup(passed, 1)
    up = regroup(turn_three, 0)

    inside = lambda at, size, n: jnp.where(
        ((at == 0) & (jnp.arange(6) == 0)) | ((at == n - 1) & (jnp.arange(6) == 5)), 0.0, 1.0
    )
    scale = 8.0 / (volume.shape[1] * nx)
    edge = jnp.concatenate(
        [inside(gx, 6, nx), inside(gy, 6, ny), jnp.full((4,), scale)]
    ).astype(F32)

    p_one, d_one, s_two = call(
        forward_one,
        [((224, 18432), BF16), ((12, 16, 1536), F32), ((6, 6, 96, 128), BF16)],
        [sm] + [vm] * 6 + [pl.ANY],
        [((14, 14, 24, 128), F32)],
        cost=10**7,
    )(edge, xlo, own, xhi, ylo, yhi, left_one, turn_two)
    p_two, d_two, mapped = call(
        forward_two,
        [((880, 2048), BF16), ((4, 32, 512), F32), ((32, 128), F32)],
        [sm] + [vm] * 2 + [pl.ANY],
        cost=10**7,
    )(place, s_two, left_two, turn_three)
    (sums,) = call(
        backward,
        [((128, 128), F32)],
        [sm, sm] + [vm] * 6,
        [((432, 2048), F32), ((96, 21504), BF16)],
        cost=10**7,
    )(place, edge, p_one, d_one, p_two, d_two, left_back, up)

    slots = mapped
    for bit in range(4):
        kept, sent = parts_of(slots, bit)
        got = flip(jnp.concatenate([sums, sent.reshape(16, 128)], axis=0), "gy", FLIPS[bit])
        sums = sums + got[0:128]
        slots = joined(kept, got[128:144])
    sums = sums + flip(sums, "gx", 4)
    sums = sums + flip(sums, "gx", 1)
    other = flip(sums, "gx", 3)

    pooled, gk1, gb1, gk2, gb2 = call(
        finish,
        [((2, 2, 1024), F32), ((27, 4, 16), F32), ((1, 16), F32), ((27, 16, 32), F32), ((1, 32), F32)],
        [sm] + [vm] * 3,
    )(place, sums, other, slots)
    gk1 = jnp.transpose(gk1.reshape(3, 3, 3, 4, 16), (4, 3, 0, 1, 2))
    gk2 = jnp.transpose(gk2.reshape(3, 3, 3, 16, 32), (4, 3, 0, 1, 2))
    return (pooled, gk1, gb1[0], gk2, gb2[0])


def solution(mesh):
    in_specs = (P(None, "gx", "gy", None), P(), P(), P(), P(), P("gy", "gx", None))
    out_specs = (P("gy", "gx", None), P(), P(), P(), P())
    return jax.shard_map(
        on_device, mesh=mesh, in_specs=in_specs, out_specs=out_specs, check_vma=False
    )
```
